256 devices in a mesh: wide: 64 (over y, z_hi, x, core), narrow: 4 (over z_lo).
Axes of the slice: x: 4, y: 4, z: 8 (z_hi: 2, z_lo: 4; z = z_hi * 4 + z_lo), core: 2. Of those that a mesh axis runs over, the one named last changes fastest.
Arguments:
- frames: bfloat16 [262144, 512], P(('wide', 'narrow')), may hold values from -6 to 6
- codebook: bfloat16 [262144, 512], P(('wide', 'narrow')), may hold values from -6 to 6
- linear_map: bfloat16 [512, 512], replicated, may hold values from -0.25 to 0.25
- code_tile: int32 [262144, 1], P(('wide', 'narrow')), may hold values from 0 to 255; in each aligned block of 1024 rows (0 to 1023, 1024 to 2047, ...) at most 8 rows name the same one
- code_offset: int32 [262144], P(('wide', 'narrow')), may hold values from 0 to 1023
- reinit_source: int32 [262144], P(('wide', 'narrow')), may hold values from 0 to 4095
Outputs:
- commitment: float32 [262144], P(('wide', 'narrow'))
- nearest: float32 [262144], P(('wide', 'narrow'))
- map_gradient: float32 [512, 512], P('wide')
- new_codebook: bfloat16 [262144, 512], P(('wide', 'narrow'))
The draws below stay inside these ranges and needn't reach their ends.
Inputs may be any that keep to these rules, and one draw needn't show every extreme that they name: `code_tile`: among the 1024 frames of one device no tile is named by more than 8 frames, a bound that some block reaches.
All inputs are finite; a program needn't handle non-finite values.
Results may differ from the reference program's by a relative error of at most 0.0024.
Values may be sent and summed in bfloat16 or wider, within the bound.
A program may use at most 64 MiB of HBM per device.

```python
import math
import jax
import jax.numpy as jnp
import numpy as np
from jax import lax

D = 512
CODE_DEV = 1024
FR_DEV = 1024
CAP = 8
CODES = 262144
FRAMES = 262144
PANEL = 4096
GROUP = 4096
N_WIDE = 64
N_NARROW = 4


def plant(entries, own_key, low, top_value):
    dims = entries.shape
    place = [jax.random.randint(jax.random.fold_in(own_key, axis), (), 0, dims[axis]) for axis in range(len(dims))]
    entries = entries.at[tuple(place)].set(low)
    longest = dims.index(max(dims))
    place[longest] = (place[longest] + 1) % dims[longest]
    return entries.at[tuple(place)].set(top_value)


def levels(rng, dims, cuts, smallest, high):
    loudness = 1.0
    for dim, blocks in cuts:
        draws = jax.random.uniform(jax.random.fold_in(jax.random.fold_in(rng, 6), dim), (blocks,), jnp.float32, smallest / len(cuts), high / len(cuts))
        loudness = loudness * jnp.repeat(jnp.exp(draws), dims[dim] // blocks).reshape((-1,) + (1,) * (len(dims) - 1 - dim))
    return loudness


def assign_block(rng, own, number, rows, number_of, top, limit, slope):
    order = jax.random.permutation(rng, number_of)
    packed, ordinary = shares(number_of, rows * top, limit, slope, True), shares(number_of, rows * top, limit, slope, False)
    places = jnp.arange(number_of)

    def named(lengths, offset_by):
        used = int((lengths > 0).sum())
        fixed = max(1, used // 4)
        moved = fixed + (places - fixed + offset_by * (used - fixed)) % max(1, number_of - fixed)
        return jnp.zeros((number_of,), jnp.int32).at[order[jnp.where(places < fixed, places, moved)]].set(jnp.asarray(lengths, jnp.int32))

    lengths = jnp.where(number % 4 == 0, named(packed, number // 4), named(ordinary, number - number // 4 - 1))
    mixed = jax.random.permutation(jax.random.fold_in(own, 3), number_of)
    giver, sink = mixed[0:number_of // 2 * 2:2], mixed[1:number_of // 2 * 2:2]
    room = jnp.minimum(lengths[giver] - 1, limit - lengths[sink]) // 2
    room = jnp.where((giver == order[0]) | (sink == order[0]) | (lengths[sink] == 0), 0, jnp.maximum(room, 0))
    moved = jax.random.randint(jax.random.fold_in(own, 4), (number_of // 2,), 0, 1 << 20) % (room + 1)
    lengths = lengths.at[giver].add(-moved).at[sink].add(moved)
    items = jnp.searchsorted(jnp.cumsum(lengths), jnp.arange(rows * top), side="right").astype(jnp.int32)
    table = items.reshape(top, rows).T
    table = table[jax.random.permutation(jax.random.fold_in(own, 1), rows)]
    offset_by = jax.random.randint(jax.random.fold_in(own, 2), (rows, 1), 0, top)
    return jnp.take_along_axis(table, (jnp.arange(top)[None, :] + offset_by) % top, axis=1)


def shares(number_of, total, limit, lean, full):
    portions = [(1 << 20) // math.isqrt(standing ** lean) + 1 for standing in range(1, number_of + 1)]
    largest = limit if full else min(limit, max(-(-total // number_of), total * portions[0] // sum(portions)))
    least = 1 if total - largest >= number_of - 1 else 0
    holding, rest = [largest] + [least] * (number_of - 1), total - largest - least * (number_of - 1)
    while rest > 0:
        movable = [i for i in range(1, number_of) if holding[i] < largest] or [i for i in range(1, number_of) if holding[i] < limit]
        whole, left = sum([portions[i] for i in movable]), rest
        for i in movable:
            addition = min(limit - holding[i], max(1, left * portions[i] // whole), rest)
            holding[i] = holding[i] + addition
            rest = rest - addition
    return np.array(holding)


def scatter_about(rng, shape, spread, bound, shards=(), held_as=jnp.bfloat16):
    array = spread * jax.random.normal(rng, shape, jnp.float32)
    if shards:
        array = array * levels(rng, shape, shards, -0.22, 0.18)
    return jnp.clip(array, -bound, bound).astype(held_as)


def setup_inputs(seed: int = 0) -> dict:
    keys = jax.random.split(jax.random.key(seed), 7)
    frames = scatter_about(keys[0], (FRAMES, D), 1.0, 6.0, ((0, 256),))
    codebook = scatter_about(keys[1], (CODES, D), 1.0, 6.0, ((0, 256),))
    linear_map = scatter_about(keys[2], (D, D), D ** -0.5, 0.25)
    code_tile_keys = jax.random.split(jax.random.fold_in(keys[3], 1), FRAMES // FR_DEV)
    code_tile_turns = jax.random.permutation(jax.random.fold_in(keys[3], 3), FRAMES // FR_DEV)
    code_tile = jax.vmap(lambda own, number: assign_block(jax.random.fold_in(keys[3], 2), own, number, FR_DEV, N_WIDE * N_NARROW, 1, CAP, 1))(code_tile_keys, code_tile_turns).reshape((FRAMES, 1))
    code_offset = plant(jax.random.randint(keys[4], (FRAMES,), 0, CODE_DEV), jax.random.fold_in(keys[4], 1), 0, CODE_DEV - 1).astype(jnp.int32)
    reinit_source = plant(jax.random.randint(keys[5], (CODES,), 0, GROUP), jax.random.fold_in(keys[5], 1), 0, GROUP - 1).astype(jnp.int32)
    return dict(frames=frames, codebook=codebook, linear_map=linear_map, code_tile=code_tile, code_offset=code_offset, reinit_source=reinit_source)


def slot_rank(targets, device_count):
    blocks = targets.reshape(device_count, FR_DEV)

    def rank_block(block):
        matches = block[:, None] == block[None, :]
        before = jnp.arange(FR_DEV, dtype=jnp.int32)[None, :] < jnp.arange(FR_DEV, dtype=jnp.int32)[:, None]
        return lax.optimization_barrier(jnp.sum((matches & before).astype(jnp.int32), axis=1))
    return jax.vmap(rank_block)(blocks).reshape(-1)

def reference(frames, codebook, linear_map, code_tile, code_offset, reinit_source):
    device_count = N_WIDE * N_NARROW
    targets = code_tile.reshape(-1).astype(jnp.int32)
    assigned = targets * CODE_DEV + code_offset
    ranking = slot_rank(targets, device_count)
    senders = jnp.arange(FRAMES, dtype=jnp.int32) // FR_DEV
    tile_slots = device_count * CAP
    position = targets * tile_slots + senders * CAP + ranking
    frame_ids = jnp.arange(FRAMES, dtype=jnp.int32)
    table = jnp.full((device_count * tile_slots,), -1, jnp.int32).at[position].set(frame_ids)
    table = table.reshape(device_count, tile_slots)

    def tile_work(inputs):
        tile_index, members = inputs
        tile_codes = lax.dynamic_slice_in_dim(codebook, (tile_index * CODE_DEV).astype(jnp.int32), CODE_DEV, 0)
        tile_effective = jnp.dot(tile_codes, linear_map, preferred_element_type=jnp.float32).astype(jnp.bfloat16)
        picked = frames[jnp.maximum(members, 0)]
        picked_f = picked.astype(jnp.float32)
        effective_f = tile_effective.astype(jnp.float32)
        cross = jnp.dot(picked, tile_effective.T, preferred_element_type=jnp.float32)
        frame_norm = lax.optimization_barrier(jnp.sum(picked_f * picked_f, axis=1))
        code_norm = lax.optimization_barrier(jnp.sum(effective_f * effective_f, axis=1))
        return lax.optimization_barrier(jnp.min(frame_norm[:, None] - 2.0 * cross + code_norm[None, :], axis=1)) / D
    tile_minima = lax.map(tile_work, (jnp.arange(device_count, dtype=jnp.int32), table))
    nearest = tile_minima.reshape(-1)[position]
    chosen = codebook[assigned]
    quantized = jnp.dot(chosen, linear_map, preferred_element_type=jnp.float32).astype(jnp.bfloat16).astype(jnp.float32)
    frames_f = frames.astype(jnp.float32)
    commitment = lax.optimization_barrier(jnp.sum((frames_f - quantized) ** 2, axis=1)) / D
    difference = (quantized - frames_f).astype(jnp.bfloat16)
    map_gradient = jnp.dot(chosen.T, difference, preferred_element_type=jnp.float32) * (2.0 / jnp.sqrt(jnp.float32(FRAMES)))
    usage = jnp.zeros((CODES,), jnp.int32).at[assigned].add(1)
    panels = jnp.arange(CODES, dtype=jnp.int32) // PANEL
    sources = panels * GROUP + reinit_source
    new_codebook = jnp.where((usage == 0)[:, None], frames[sources], codebook)
    return (commitment, nearest, map_gradient, new_codebook)
```

```python
import functools

import jax
import jax.numpy as jnp
from jax import lax
from jax.experimental import pallas as pl
from jax.experimental.pallas import tpu as pltpu
from jax.sharding import PartitionSpec as P

MESH = pl.DeviceIdType.MESH
F32 = jnp.float32
BF16 = jnp.bfloat16

ROWS = 1024
WIDTH = 512
DEVICES = 256
CAP = 8
GROUPS = 8
PER_GROUP = DEVICES // GROUPS
SLOTS = PER_GROUP * CAP
HALF = WIDTH // 2
BLOCK = 2 * CAP
FETCH = 320
SEND_AT = 2


def coordinates():
    wide = lax.axis_index("wide")
    narrow = lax.axis_index("narrow")
    return (wide // 2) % 4, wide // 16, ((wide // 8) % 2) * 4 + narrow, wide % 2


def device(x, y, z, core):
    return {"wide": ((y * 2 + z // 4) * 4 + x) * 2 + core, "narrow": lax.rem(z, 4)}


def ahead(step, here):
    x, y, z, core = here
    return device(
        lax.rem(x + (step // 16) % 4, 4),
        lax.rem(y + step // 64, 4),
        lax.rem(z + step % 8, 8),
        lax.rem(core + (step // 8) % 2, 2),
    )


def behind(step, here):
    x, y, z, core = here
    return device(
        lax.rem(x + 4 - (step // 16) % 4, 4),
        lax.rem(y + 4 - step // 64, 4),
        lax.rem(z + 8 - step % 8, 8),
        lax.rem(core + (step // 8) % 2, 2),
    )


def iota(shape, dim):
    return lax.broadcasted_iota(jnp.int32, shape, dim)


def nn(a, b):
    return lax.dot_general(a, b, (((1,), (0,)), ((), ())), preferred_element_type=F32)


def nt(a, b):
    return lax.dot_general(a, b, (((1,), (1,)), ((), ())), preferred_element_type=F32)


def tn(a, b):
    return lax.dot_general(a, b, (((0,), (0,)), ((), ())), preferred_element_type=F32)


def one(mask):
    return jnp.where(mask, 1.0, 0.0).astype(BF16)


def remote(src, dst, send, recv, target):
    return pltpu.make_async_remote_copy(
        src_ref=src, dst_ref=dst, send_sem=send, recv_sem=recv, device_id=target, device_id_type=MESH
    )


def drain(ref, sem):
    pltpu.make_async_copy(ref, ref, sem).wait()


def fetch_ranks(source, before):
    owner = source >> 10
    owners = one(owner == iota((16, ROWS), 0))
    counts = nn(owners, before)
    return jnp.sum(owners.astype(F32) * counts, axis=0, keepdims=True).astype(jnp.int32)


def step_kernel(
    frames, codebook, linear_map, tile, offset, source,
    commit_out, near_out, grad_out, fresh_out, used_out, over_out,
    outgoing, arrived, labels_out, labels_in, results_out, results_in,
    before, effective, code_norm, place, usage, total,
    half_in, half_sum, plane_in, plane_sum, column_in,
    asked, rows_out, rows_in, fresh,
    data_send, data_recv, label_send, label_recv, result_send, result_recv,
    half_send, half_recv, plane_send, plane_recv, column_send, column_recv,
    ask_send, ask_recv, row_send, row_recv, ready,
):
    here = coordinates()
    x, y, z, core = here
    narrow = lax.axis_index("narrow")

    barrier = pltpu.get_barrier_semaphore()

    def greet(sem, first, last, stride):
        def body(step, carry):
            pl.semaphore_signal(sem, inc=1, device_id=ahead(step * stride, here), device_id_type=MESH)
            return carry

        lax.fori_loop(first, last, body, 0)

    greet(barrier, 1, 8, 1)
    greet(barrier, 1, 32, 8)

    before[...] = one(iota((ROWS, ROWS), 0) < iota((ROWS, ROWS), 1))
    named = tile[...]
    wide = named >> 2
    depth = ((wide >> 3) & 1) * 4 + (named & 3)
    step_of = (
        ((depth + 8 - z) & 7)
        + 8 * (((wide & 1) + 2 - core) & 1)
        + 16 * ((((wide >> 1) & 3) + 4 - x) & 3)
        + 64 * (((wide >> 4) + 4 - y) & 3)
    )
    chosen_step = one(step_of == iota((DEVICES, ROWS), 0))
    earlier = nn(chosen_step, before[...])
    rank = jnp.sum(chosen_step.astype(F32) * earlier, axis=0, keepdims=True).astype(jnp.int32)
    place[0:1, :] = step_of
    place[1:2, :] = rank
    place[2:3, :] = step_of * CAP + rank
    fetch_rank = fetch_ranks(source[...], before[...])
    place[3:4, :] = fetch_rank
    far = (source[...] >> 10) != narrow
    over = jnp.max(jnp.where(far & (fetch_rank >= FETCH), 1.0, 0.0), axis=1, keepdims=True)

    label = offset[...] + 1
    at_rank = rank == iota((128, ROWS), 0)
    high = jnp.where(at_rank, (label >> 5).astype(F32), 0.0).astype(BF16)
    low = jnp.where(at_rank, (label & 31).astype(F32), 0.0).astype(BF16)
    marks = 32.0 * nt(chosen_step, high) + nt(chosen_step, low)
    marks = jnp.where(iota((DEVICES, 128), 1) == 127, over, marks)
    labels_out[...] = marks.reshape(DEVICES, 1, 128)

    def dispatch(group, carry):
        slots = iota((SLOTS, ROWS), 0) + group * SLOTS
        picked = nn(one(place[2:3, :] == slots), frames[...])
        left = picked[:, :HALF].reshape(PER_GROUP, 1, CAP, HALF)
        right = picked[:, HALF:].reshape(PER_GROUP, 1, CAP, HALF)
        block = jnp.concatenate([left, right], axis=1).reshape(2 * SLOTS, HALF)
        outgoing[pl.ds(pl.multiple_of(group * 2 * SLOTS, 2 * SLOTS), 2 * SLOTS), :] = block.astype(BF16)
        return carry

    lax.fori_loop(0, GROUPS, dispatch, 0)

    pl.semaphore_wait(barrier, 38)
    greet(ready, 1, 8, 1)
    pl.semaphore_wait(ready, 7)

    for j in range(3):
        target = {"narrow": lax.rem(narrow + j + 1, 4)}
        remote(source, asked.at[j], ask_send, ask_recv.at[j], target).start()

    own_data = pltpu.make_async_copy(outgoing.at[pl.ds(0, BLOCK)], arrived.at[pl.ds(0, BLOCK)], data_recv.at[0])
    own_data.start()
    own_label = pltpu.make_async_copy(labels_out.at[0], labels_in.at[0], label_recv.at[0])
    own_label.start()

    def send(step, carry):
        target = ahead(step, here)
        group = step // PER_GROUP
        rows = pl.ds(pl.multiple_of(step * BLOCK, BLOCK), BLOCK)
        remote(labels_out.at[step], labels_in.at[step], label_send, label_recv.at[group], target).start()
        remote(outgoing.at[rows], arrived.at[rows], data_send, data_recv.at[group], target).start()
        return carry

    lax.fori_loop(1, DEVICES, send, 0)

    eff = nn(codebook[...], linear_map[...]).astype(BF16)
    effective[...] = eff
    eff_f = eff.astype(F32)
    norms = jnp.sum(eff_f * eff_f, axis=1, keepdims=True)
    code_norm[...] = jnp.transpose(jnp.broadcast_to(norms, (ROWS, 128)))[0:1, :]
    usage[...] = jnp.zeros_like(usage)
    total[...] = jnp.zeros_like(total)

    for j in range(3):
        drain(asked.at[j], ask_recv.at[j])
        wanted = asked[j]
        order = fetch_ranks(wanted, before[...])
        mine = ((wanted >> 10) == narrow) & (order == iota((FETCH, ROWS), 0))
        index = jnp.sum(jnp.where(mine, (wanted & 1023).astype(F32), 0.0), axis=1, keepdims=True)
        rows = one(index.astype(jnp.int32) == iota((FETCH, ROWS), 1))
        rows_out[j] = nn(rows, frames[...]).astype(BF16)

    def work(group, carry):
        rows = pl.ds(pl.multiple_of(group * 2 * SLOTS, 2 * SLOTS), 2 * SLOTS)
        messages = pl.ds(group * PER_GROUP, PER_GROUP)
        drain(labels_in.at[messages], label_recv.at[group])
        drain(arrived.at[rows], data_recv.at[group])

        @pl.when(group == SEND_AT)
        def _():
            for j in range(3):
                target = {"narrow": lax.rem(narrow + 3 - j, 4)}
                remote(rows_out.at[j], rows_in.at[j], row_send, row_recv.at[j], target).start()

        parts = arrived[rows, :].astype(F32).reshape(PER_GROUP, 2, CAP, HALF)
        taken_f = jnp.concatenate(
            [parts[:, 0].reshape(SLOTS, HALF), parts[:, 1].reshape(SLOTS, HALF)], axis=1
        )
        taken = taken_f.astype(BF16)
        spread = jnp.broadcast_to(labels_in[messages], (PER_GROUP, CAP, 128)).reshape(SLOTS, 128)
        row_rank = iota((SLOTS, 128), 0) & (CAP - 1)
        lane = iota((SLOTS, 128), 1)
        mark = jnp.sum(jnp.where(lane == row_rank, spread, 0.0), axis=1, keepdims=True)
        code = mark.astype(jnp.int32) - 1
        chosen_mask = code == iota((SLOTS, ROWS), 1)
        selector = one(chosen_mask)
        usage[...] += jnp.sum(jnp.where(chosen_mask, 1.0, 0.0), axis=0, keepdims=True)
        quantized = nn(selector, effective[...])
        chosen = nn(selector, codebook[...]).astype(BF16)
        gap = quantized - taken_f
        commitment = jnp.sum(gap * gap, axis=1, keepdims=True) * (1.0 / WIDTH)
        cross = nt(taken, effective[...])
        least = jnp.min(code_norm[...] - 2.0 * cross, axis=1, keepdims=True)
        nearest = (jnp.sum(taken_f * taken_f, axis=1, keepdims=True) + least) * (1.0 / WIDTH)
        total[...] += tn(chosen, gap.astype(BF16)).reshape(total.shape)
        back = jnp.where(lane == row_rank, commitment, 0.0) + jnp.where(lane == row_rank + CAP, nearest, 0.0)
        results_out[messages] = jnp.sum(back.reshape(PER_GROUP, CAP, 128), axis=1, keepdims=True)

        def give(step, carry):
            @pl.when(step > 0)
            def _():
                remote(
                    results_out.at[step], results_in.at[step], result_send, result_recv, behind(step, here)
                ).start()

            @pl.when(step == 0)
            def _():
                pltpu.make_async_copy(results_out.at[0], results_in.at[0], result_recv).start()

            return carry

        lax.fori_loop(group * PER_GROUP, (group + 1) * PER_GROUP, give, 0)
        return carry

    lax.fori_loop(0, GROUPS, work, 0)

    to_pair = remote(total.at[:, :, :, 1 - core], half_in, half_send, half_recv, device(x, y, z, 1 - core))
    to_pair.start()

    wanted = source[...]
    mine = ((wanted >> 10) == narrow) & ((wanted & 1023) == iota((ROWS, ROWS), 0))
    fresh[...] = tn(one(mine), frames[...])

    to_pair.wait()
    half_sum[...] = total[:, :, :, core] + half_in[...]
    for step in range(1, 16):
        x2 = lax.rem(x + step % 4, 4)
        y2 = lax.rem(y + step // 4, 4)
        remote(
            half_sum.at[y2, :, x2], plane_in.at[step - 1], plane_send, plane_recv, device(x2, y2, z, core)
        ).start()

    drain(results_in, result_recv)
    returned = results_in[...].reshape(DEVICES, 128)
    steps = one(place[0:1, :] == iota((DEVICES, ROWS), 0))
    first = returned.astype(BF16)
    rest = returned - first.astype(F32)
    second = rest.astype(BF16)
    third = (rest - second.astype(F32)).astype(BF16)
    home = tn(first, steps) + tn(second, steps) + tn(third, steps)
    here_rank = place[1:2, :] == iota((CAP, ROWS), 0)
    commit_out[...] = jnp.sum(jnp.where(here_rank, home[0:CAP], 0.0), axis=0, keepdims=True)
    near_out[...] = jnp.sum(jnp.where(here_rank, home[CAP : 2 * CAP], 0.0), axis=0, keepdims=True)

    drain(plane_in, plane_recv)
    plane_sum[...] = half_sum[y, :, x] + jnp.sum(plane_in[...], axis=0)
    for step in range(1, 8):
        z2 = lax.rem(z + step, 8)
        remote(
            plane_sum.at[z2 // 4], column_in.at[step - 1], column_send, column_recv, device(x, y, z2, core)
        ).start()

    for j in range(3):
        drain(rows_in.at[j], row_recv.at[j])
        peer = lax.rem(narrow + j + 1, 4)
        wanted = source[...]
        asked_for = ((wanted >> 10) == peer) & (place[3:4, :] == iota((FETCH, ROWS), 0))
        fresh[...] += tn(one(asked_for), rows_in[j])

    used = usage[...]
    used_out[...] = used
    used_column = jnp.transpose(jnp.broadcast_to(used, (128, ROWS)))[:, 0:1]
    fresh_out[...] = jnp.where(used_column > 0.0, codebook[...].astype(F32), fresh[...]).astype(BF16)
    over_out[...] = jnp.max(labels_in[...], axis=0)

    drain(column_in, column_recv)
    grad_out[...] = (plane_sum[z // 4] + jnp.sum(column_in[...], axis=0)) * (2.0 / 512.0)

    sent = pl.ds(BLOCK, (DEVICES - 1) * BLOCK)
    messages = pl.ds(1, DEVICES - 1)
    drain(outgoing.at[sent], data_send)
    drain(labels_out.at[messages], label_send)
    drain(results_out.at[messages], result_send)
    drain(plane_in, plane_send)
    drain(column_in, column_send)
    drain(asked, ask_send)
    drain(rows_out, row_send)


def exchange(frames, codebook, linear_map, tile, offset, source):
    vmem = pl.BlockSpec(memory_space=pltpu.VMEM)
    dma = pltpu.SemaphoreType.DMA
    return pl.pallas_call(
        step_kernel,
        out_shape=[
            jax.ShapeDtypeStruct((1, ROWS), F32),
            jax.ShapeDtypeStruct((1, ROWS), F32),
            jax.ShapeDtypeStruct((CAP, WIDTH), F32),
            jax.ShapeDtypeStruct((ROWS, WIDTH), BF16),
            jax.ShapeDtypeStruct((1, ROWS), F32),
            jax.ShapeDtypeStruct((1, 128), F32),
        ],
        in_specs=[vmem] * 6,
        out_specs=[vmem] * 6,
        scratch_shapes=[
            pltpu.VMEM((DEVICES * BLOCK, HALF), BF16),
            pltpu.VMEM((DEVICES * BLOCK, HALF), BF16),
            pltpu.VMEM((DEVICES, 1, 128), F32),
            pltpu.VMEM((DEVICES, 1, 128), F32),
            pltpu.VMEM((DEVICES, 1, 128), F32),
            pltpu.VMEM((DEVICES, 1, 128), F32),
            pltpu.VMEM((ROWS, ROWS), BF16),
            pltpu.VMEM((ROWS, WIDTH), BF16),
            pltpu.VMEM((1, ROWS), F32),
            pltpu.VMEM((8, ROWS), jnp.int32),
            pltpu.VMEM((1, ROWS), F32),
            pltpu.VMEM((4, 2, 4, 2, 8, WIDTH), F32),
            pltpu.VMEM((4, 2, 4, 8, WIDTH), F32),
            pltpu.VMEM((4, 2, 4, 8, WIDTH), F32),
            pltpu.VMEM((15, 2, 8, WIDTH), F32),
            pltpu.VMEM((2, 8, WIDTH), F32),
            pltpu.VMEM((7, 8, WIDTH), F32),
            pltpu.VMEM((3, 1, ROWS), jnp.int32),
            pltpu.VMEM((3, FETCH, WIDTH), BF16),
            pltpu.VMEM((3, FETCH, WIDTH), BF16),
            pltpu.VMEM((ROWS, WIDTH), F32),
            dma, dma((GROUPS,)), dma, dma((GROUPS,)), dma, dma,
            dma, dma, dma, dma, dma, dma,
            dma, dma((3,)), dma, dma((3,)), pltpu.SemaphoreType.REGULAR,
        ],
        compiler_params=pltpu.CompilerParams(
            collective_id=0, has_side_effects=True, vmem_limit_bytes=52 * 2**20
        ),
    )(frames, codebook, linear_map, tile, offset, source)


def shards(frames, codebook, linear_map, code_tile, code_offset, reinit_source):
    commitment, nearest, gradient, fresh, used, over = exchange(
        frames,
        codebook,
        linear_map,
        code_tile.reshape(1, ROWS),
        code_offset.reshape(1, ROWS),
        reinit_source.reshape(1, ROWS),
    )

    def whole_gather():
        group = lax.all_gather(frames, "narrow", axis=0, tiled=True)
        return jnp.where(used.reshape(ROWS, 1) > 0.0, codebook, group[reinit_source])

    new_codebook = lax.cond(over[0, 127] > 0.0, whole_gather, lambda: fresh)
    return commitment.reshape(ROWS), nearest.reshape(ROWS), gradient, new_codebook


def solution(mesh):
    placed = (
        P(("wide", "narrow"), None),
        P(("wide", "narrow"), None),
        P(),
        P(("wide", "narrow"), None),
        P(("wide", "narrow")),
        P(("wide", "narrow")),
    )
    return jax.shard_map(
        shards,
        mesh=mesh,
        in_specs=placed,
        out_specs=(
            P(("wide", "narrow")),
            P(("wide", "narrow")),
            P("wide", None),
            P(("wide", "narrow"), None),
        ),
        check_vma=False,
    )
```

```python
import functools

import jax
import jax.numpy as jnp
from jax import lax
from jax.experimental import pallas as pl
from jax.experimental.pallas import tpu as pltpu
from jax.sharding import PartitionSpec as P

MESH = pl.DeviceIdType.MESH
F32 = jnp.float32
BF16 = jnp.bfloat16

ROWS = 1024
WIDTH = 512
DEVICES = 256
CAP = 8
GROUPS = 8
PER_GROUP = DEVICES // GROUPS
SLOTS = PER_GROUP * CAP
HALF = WIDTH // 2
BLOCK = 2 * CAP
FETCH = 208
SEND_AT = 7
PLANE = 32
DEPTH = 8
PLANE_GROUP = PLANE // GROUPS
FETCHED = 640


def coordinates():
    wide = lax.axis_index("wide")
    narrow = lax.axis_index("narrow")
    return (wide // 2) % 4, wide // 16, ((wide // 8) % 2) * 4 + narrow, wide % 2


def device(x, y, z, core):
    return {"wide": ((y * 2 + z // 4) * 4 + x) * 2 + core, "narrow": lax.rem(z, 4)}


def plane_index(step, here, sign):
    x, y, _, core = here
    x2 = lax.rem(x + 4 + sign * lax.rem(step // 2, 4), 4)
    y2 = lax.rem(y + 4 + sign * (step // 8), 4)
    return y2 * 16 + x2 * 2 + lax.rem(core + lax.rem(step, 2), 2)


def column_index(step, here, sign):
    z2 = lax.rem(here[2] + 8 + sign * step, 8)
    return (z2 // 4) * 8, lax.rem(z2, 4)


def iota(shape, dim):
    return lax.broadcasted_iota(jnp.int32, shape, dim)


def nn(a, b):
    return lax.dot_general(a, b, (((1,), (0,)), ((), ())), preferred_element_type=F32)


def nt(a, b):
    return lax.dot_general(a, b, (((1,), (1,)), ((), ())), preferred_element_type=F32)


def tn(a, b):
    return lax.dot_general(a, b, (((0,), (0,)), ((), ())), preferred_element_type=F32)


def one(mask):
    return jnp.where(mask, 1.0, 0.0).astype(BF16)


def remote(src, dst, send, recv, target):
    return pltpu.make_async_remote_copy(
        src_ref=src, dst_ref=dst, send_sem=send, recv_sem=recv, device_id=target, device_id_type=MESH
    )


def drain(ref, sem):
    pltpu.make_async_copy(ref, ref, sem).wait()


def fetch_ranks(source, before):
    owner = source >> 10
    owners = one(owner == iota((16, ROWS), 0))
    counts = nn(owners, before)
    return jnp.sum(owners.astype(F32) * counts, axis=0, keepdims=True).astype(jnp.int32)


def step_kernel(
    frames_in, codebook_in, linear_in, tile_in, offset_in, source_in,
    commit_out, near_out, grad_out, fresh_out, used_out, over_out,
    frames, codebook, linear_map, tile, offset, source, wanted_here,
    outgoing, arrived, labels_out, labels_mid, labels_in, results_out, results_mid, results_pack, results_in,
    before, effective, code_norm, place, total,
    half_in, half_sum, plane_in, plane_sum, column_in,
    asked, rows_out, rows_in, picks, fresh,
    load, data_send, data_recv, column_label_send, column_label_recv, plane_label_send, plane_label_recv,
    plane_result_send, plane_result_recv, column_result_send, column_result_recv,
    half_send, half_recv, plane_send, plane_recv, column_send, column_recv,
    ask_send, ask_recv, row_send, row_recv,
):
    here = coordinates()
    x, y, z, core = here
    narrow = lax.axis_index("narrow")

    loads = [
        pltpu.make_async_copy(src, dst, load.at[i])
        for i, (src, dst) in enumerate(
            (
                (tile_in, tile),
                (offset_in, offset),
                (source_in, source),
                (frames_in, frames),
                (codebook_in, codebook),
                (linear_in, linear_map),
            )
        )
    ]
    for copy in loads:
        copy.start()

    columns = [column_index(step, here, 1) for step in range(DEPTH)]
    plane_here = plane_index(0, here, 1)

    def target(base, step):
        return {"wide": base + columns[step][0], "narrow": columns[step][1]}

    barrier = pltpu.get_barrier_semaphore()
    for step in range(1, DEPTH):
        pl.semaphore_signal(barrier, inc=1, device_id=target(plane_here, step), device_id_type=MESH)

    def greet(step, carry):
        pl.semaphore_signal(
            barrier, inc=1, device_id=target(plane_index(step, here, 1), 0), device_id_type=MESH
        )
        return carry

    lax.fori_loop(1, PLANE, greet, 0)

    before[...] = one(iota((ROWS, ROWS), 0) < iota((ROWS, ROWS), 1))
    for copy in loads[:3]:
        copy.wait()
    named = tile[...]
    wide = named >> 2
    depth = ((wide >> 3) & 1) * 4 + (named & 3)
    step_of = (
        ((depth + 8 - z) & 7)
        + 8 * (((wide & 1) + 2 - core) & 1)
        + 16 * ((((wide >> 1) & 3) + 4 - x) & 3)
        + 64 * (((wide >> 4) + 4 - y) & 3)
    )
    chosen_step = one(step_of == iota((DEVICES, ROWS), 0))
    earlier = nn(chosen_step, before[...])
    rank = jnp.sum(chosen_step.astype(F32) * earlier, axis=0, keepdims=True).astype(jnp.int32)
    place[0:1, :] = step_of
    place[1:2, :] = rank
    place[2:3, :] = step_of * CAP + rank

    label = offset[...] + 1
    at_lane = (step_of >> 3) * CAP + rank == iota((PLANE * CAP, ROWS), 0)
    high = jnp.where(at_lane, (label >> 5).astype(F32), 0.0).astype(BF16)
    low = jnp.where(at_lane, (label & 31).astype(F32), 0.0).astype(BF16)
    chosen_depth = one((step_of & 7) == iota((16, ROWS), 0))
    marks = (32.0 * nt(chosen_depth, high) + nt(chosen_depth, low))[:DEPTH]
    labels_out[:, 0] = marks[:, :128].reshape(DEPTH, 1, 128)
    labels_out[:, 1] = marks[:, 128:].reshape(DEPTH, 1, 128)
    labels_mid[0] = labels_out[0]
    loads[3].wait()

    def dispatch(group):
        slots = iota((SLOTS, ROWS), 0) + group * SLOTS
        picked = nn(one(place[2:3, :] == slots), frames[...])
        left = picked[:, :HALF].reshape(PER_GROUP, 1, CAP, HALF)
        right = picked[:, HALF:].reshape(PER_GROUP, 1, CAP, HALF)
        block = jnp.concatenate([left, right], axis=1).reshape(2 * SLOTS, HALF)
        outgoing[pl.ds(pl.multiple_of(group * 2 * SLOTS, 2 * SLOTS), 2 * SLOTS), :] = block.astype(BF16)

    dispatch(0)

    pl.semaphore_wait(barrier, DEPTH + PLANE - 2)

    for step in range(1, DEPTH):
        remote(
            labels_out.at[step], labels_mid.at[step], column_label_send, column_label_recv,
            target(plane_here, step),
        ).start()
    drain(labels_mid.at[pl.ds(1, DEPTH - 1)], column_label_recv)

    own_label = pltpu.make_async_copy(labels_mid.at[:, 0], labels_in.at[0], plane_label_recv)
    own_label.start()

    def label_plane(step, carry):
        remote(
            labels_mid.at[:, step // 16], labels_in.at[step], plane_label_send, plane_label_recv,
            target(plane_index(step, here, 1), 0),
        ).start()
        return carry

    lax.fori_loop(1, PLANE, label_plane, 0)

    own_data = pltpu.make_async_copy(outgoing.at[pl.ds(0, BLOCK)], arrived.at[pl.ds(0, BLOCK)], data_recv.at[0])
    own_data.start()

    def send(step, first):
        base = plane_index(step, here, 1)
        start = pl.multiple_of(step * (DEPTH * BLOCK), DEPTH * BLOCK)
        for d in range(first, DEPTH):
            rows = pl.ds(start + d * BLOCK, BLOCK)
            remote(
                outgoing.at[rows], arrived.at[rows], data_send, data_recv.at[step // PLANE_GROUP], target(base, d)
            ).start()

    def send_plane(step, carry):
        send(step, 0)
        return carry

    send(0, 1)
    lax.fori_loop(1, PLANE_GROUP, send_plane, 0)

    def dispatch_and_send(group, carry):
        dispatch(group)
        lax.fori_loop(group * PLANE_GROUP, (group + 1) * PLANE_GROUP, send_plane, 0)
        return carry

    lax.fori_loop(1, GROUPS, dispatch_and_send, 0)

    drain(labels_in, plane_label_recv)
    row_rank = iota((SLOTS, 128), 0) & (CAP - 1)
    lane = iota((SLOTS, 128), 1)

    plane_step = iota((SLOTS, 128), 0) >> 6

    def codes(group):
        marks = labels_in[pl.ds(group * PLANE_GROUP, PLANE_GROUP)]
        spread = jnp.broadcast_to(marks.reshape(PER_GROUP, 1, 128), (PER_GROUP, CAP, 128)).reshape(SLOTS, 128)
        at = ((plane_step + group * PLANE_GROUP) & 15) * CAP + row_rank
        mark = jnp.sum(jnp.where(lane == at, spread, 0.0), axis=1, keepdims=True)
        return (mark.astype(jnp.int32) - 1) == iota((SLOTS, ROWS), 1)

    def count(group, used):
        return used + jnp.sum(jnp.where(codes(group), 1.0, 0.0), axis=0, keepdims=True)

    used = lax.fori_loop(0, GROUPS, count, jnp.zeros((1, ROWS), F32))
    used_out[...] = used
    wanted = jnp.where(used > 0.0, 8 * ROWS, source[...])
    wanted_here[...] = wanted
    for j in range(3):
        peer = {"narrow": lax.rem(narrow + j + 1, 4)}
        remote(wanted_here, asked.at[j], ask_send, ask_recv.at[j], peer).start()
    fetch_rank = fetch_ranks(wanted, before[...])
    far = ((wanted >> 10) != narrow) & (used == 0.0)
    over = jnp.max(jnp.where(far & (fetch_rank >= FETCH), 1.0, 0.0), axis=1, keepdims=True)
    results_out[:, DEPTH] = jnp.broadcast_to(over.reshape(1, 1, 1), (PLANE, 1, 128))

    for copy in loads[4:]:
        copy.wait()
    eff = nn(codebook[...], linear_map[...]).astype(BF16)
    effective[...] = eff
    eff_f = eff.astype(F32)
    norms = jnp.sum(eff_f * eff_f, axis=1, keepdims=True)
    code_norm[...] = jnp.transpose(jnp.broadcast_to(norms, (ROWS, 128)))[0:1, :]
    total[...] = jnp.zeros_like(total)

    for j in range(3):
        drain(asked.at[j], ask_recv.at[j])
        theirs = asked[j]
        order = fetch_ranks(theirs, before[...])
        mine = ((theirs >> 10) == narrow) & (order == iota((FETCH, ROWS), 0))
        index = jnp.sum(jnp.where(mine, (theirs & 1023).astype(F32), 0.0), axis=1, keepdims=True)
        rows = one(index.astype(jnp.int32) == iota((FETCH, ROWS), 1))
        rows_out[j] = nn(rows, frames[...]).astype(BF16)

    mine = ((wanted >> 10) == narrow) & ((wanted & 1023) == iota((ROWS, ROWS), 0))
    used_column = jnp.transpose(jnp.broadcast_to(used, (128, ROWS)))[:, 0:1]
    fresh[...] = jnp.where(used_column > 0.0, codebook[...].astype(F32), tn(one(mine), frames[...])).astype(BF16)
    asked_for = [
        jnp.where(((wanted >> 10) == lax.rem(narrow + j + 1, 4)) & (fetch_rank == iota((FETCH, ROWS), 0)), 1.0, 0.0)
        for j in range(3)
    ]
    spare = FETCHED - 3 * FETCH
    picks[...] = jnp.transpose(jnp.concatenate(asked_for + [jnp.zeros((spare, ROWS), F32)], axis=0)).astype(BF16)
    rows_in[pl.ds(3 * FETCH, spare), :] = jnp.zeros((spare, WIDTH), BF16)

    def work(group, carry):
        rows = pl.ds(pl.multiple_of(group * 2 * SLOTS, 2 * SLOTS), 2 * SLOTS)
        drain(arrived.at[rows], data_recv.at[group])

        @pl.when(group == SEND_AT)
        def _():
            for j in range(3):
                peer = {"narrow": lax.rem(narrow + 3 - j, 4)}
                remote(
                    rows_out.at[j], rows_in.at[pl.ds(j * FETCH, FETCH)], row_send, row_recv.at[j], peer
                ).start()

        parts = arrived[rows, :].astype(F32).reshape(PER_GROUP, 2, CAP, HALF)
        taken_f = jnp.concatenate(
            [parts[:, 0].reshape(SLOTS, HALF), parts[:, 1].reshape(SLOTS, HALF)], axis=1
        )
        taken = taken_f.astype(BF16)
        chosen_mask = codes(group)
        selector = one(chosen_mask)
        quantized = nn(selector, effective[...])
        chosen = nn(selector, codebook[...]).astype(BF16)
        gap = quantized - taken_f
        commitment = jnp.sum(gap * gap, axis=1, keepdims=True) * (1.0 / WIDTH)
        cross = nt(taken, effective[...])
        least = jnp.min(code_norm[...] - 2.0 * cross, axis=1, keepdims=True)
        nearest = (jnp.sum(taken_f * taken_f, axis=1, keepdims=True) + least) * (1.0 / WIDTH)
        total[...] += tn(chosen, gap.astype(BF16)).reshape(total.shape)
        at = ((plane_step + group * PLANE_GROUP) & 7) * (2 * CAP) + row_rank
        back = jnp.where(lane == at, commitment, 0.0) + jnp.where(lane == at + CAP, nearest, 0.0)
        back = jnp.sum(back.reshape(PER_GROUP, CAP, 128), axis=1, keepdims=True)
        results_out[pl.ds(group * PLANE_GROUP, PLANE_GROUP), pl.ds(0, DEPTH)] = back.reshape(PLANE_GROUP, DEPTH, 1, 128)

        def give(step):
            remote(
                results_out.at[step], results_mid.at[step], plane_result_send, plane_result_recv,
                target(plane_index(step, here, -1), 0),
            ).start()

        @pl.when(group > 0)
        def _():
            give(group * PLANE_GROUP)

        @pl.when(group == 0)
        def _():
            pltpu.make_async_copy(results_out.at[0], results_mid.at[0], plane_result_recv).start()

        for step in range(1, PLANE_GROUP):
            give(group * PLANE_GROUP + step)
        return carry

    lax.fori_loop(0, GROUPS, work, 0)

    to_pair = remote(total.at[:, :, :, 1 - core], half_in, half_send, half_recv, device(x, y, z, 1 - core))
    to_pair.start()

    to_pair.wait()
    half_sum[...] = total[:, :, :, core] + half_in[...]
    for step in range(1, 16):
        x2 = lax.rem(x + step % 4, 4)
        y2 = lax.rem(y + step // 4, 4)
        remote(
            half_sum.at[y2, :, x2], plane_in.at[step - 1], plane_send, plane_recv, device(x2, y2, z, core)
        ).start()

    drain(results_mid, plane_result_recv)
    for block in range(4):
        results_pack[:, block] = jnp.sum(results_mid[pl.ds(block * 8, 8), pl.ds(0, DEPTH)], axis=0)
    results_pack[:, 4] = jnp.broadcast_to(jnp.max(results_mid[:, DEPTH], axis=0, keepdims=True), (DEPTH, 1, 128))
    results_in[0] = results_pack[0]
    for step in range(1, DEPTH):
        offset_wide, narrow_back = column_index(step, here, -1)
        remote(
            results_pack.at[step], results_in.at[step], column_result_send, column_result_recv,
            {"wide": plane_here + offset_wide, "narrow": narrow_back},
        ).start()

    drain(plane_in, plane_recv)
    plane_sum[...] = half_sum[y, :, x] + jnp.sum(plane_in[...], axis=0)
    for step in range(1, 8):
        z2 = lax.rem(z + step, 8)
        remote(
            plane_sum.at[z2 // 4], column_in.at[step - 1], column_send, column_recv, device(x, y, z2, core)
        ).start()

    drain(results_in.at[pl.ds(1, DEPTH - 1)], column_result_recv)
    over_out[...] = jnp.max(results_in[:, 4], axis=0)
    returned = results_in[:, pl.ds(0, 4)].reshape(PLANE, 128)
    step_of = place[0:1, :]
    steps = one((step_of & 7) * 4 + (step_of >> 6) == iota((PLANE, ROWS), 0))
    first = returned.astype(BF16)
    rest = returned - first.astype(F32)
    second = rest.astype(BF16)
    third = (rest - second.astype(F32)).astype(BF16)
    home = tn(first, steps) + tn(second, steps) + tn(third, steps)
    at = ((step_of >> 3) & 7) * (2 * CAP) + place[1:2, :]
    commit_out[...] = jnp.sum(jnp.where(at == iota((128, ROWS), 0), home, 0.0), axis=0, keepdims=True)
    near_out[...] = jnp.sum(jnp.where(at + CAP == iota((128, ROWS), 0), home, 0.0), axis=0, keepdims=True)

    for j in range(3):
        drain(rows_in.at[pl.ds(j * FETCH, FETCH)], row_recv.at[j])
    fresh_out[...] = (fresh[...].astype(F32) + nn(picks[...], rows_in[...])).astype(BF16)

    drain(column_in, column_recv)
    grad_out[...] = (plane_sum[z // 4] + jnp.sum(column_in[...], axis=0)) * (2.0 / 512.0)

    sent = pl.ds(BLOCK, (DEVICES - 1) * BLOCK)
    drain(outgoing.at[sent], data_send)
    drain(labels_mid.at[pl.ds(1, DEPTH - 1)], column_label_send)
    drain(labels_in.at[pl.ds(1, PLANE - 1)], plane_label_send)
    drain(results_mid.at[pl.ds(1, PLANE - 1)], plane_result_send)
    drain(results_in.at[pl.ds(1, DEPTH - 1)], column_result_send)
    drain(plane_in, plane_send)
    drain(column_in, column_send)
    drain(asked, ask_send)
    drain(rows_out, row_send)


def exchange(frames, codebook, linear_map, tile, offset, source):
    vmem = pl.BlockSpec(memory_space=pltpu.VMEM)
    dma = pltpu.SemaphoreType.DMA
    return pl.pallas_call(
        step_kernel,
        out_shape=[
            jax.ShapeDtypeStruct((1, ROWS), F32),
            jax.ShapeDtypeStruct((1, ROWS), F32),
            jax.ShapeDtypeStruct((CAP, WIDTH), F32),
            jax.ShapeDtypeStruct((ROWS, WIDTH), BF16),
            jax.ShapeDtypeStruct((1, ROWS), F32),
            jax.ShapeDtypeStruct((1, 128), F32),
        ],
        in_specs=[pl.BlockSpec(memory_space=pl.ANY)] * 6,
        out_specs=[vmem] * 6,
        scratch_shapes=[
            pltpu.VMEM((ROWS, WIDTH), BF16),
            pltpu.VMEM((ROWS, WIDTH), BF16),
            pltpu.VMEM((WIDTH, WIDTH), BF16),
            pltpu.VMEM((1, ROWS), jnp.int32),
            pltpu.VMEM((1, ROWS), jnp.int32),
            pltpu.VMEM((1, ROWS), jnp.int32),
            pltpu.VMEM((1, ROWS), jnp.int32),
            pltpu.VMEM((DEVICES * BLOCK, HALF), BF16),
            pltpu.VMEM((DEVICES * BLOCK, HALF), BF16),
            pltpu.VMEM((DEPTH, 2, 1, 128), F32),
            pltpu.VMEM((DEPTH, 2, 1, 128), F32),
            pltpu.VMEM((PLANE, DEPTH, 1, 128), F32),
            pltpu.VMEM((PLANE, DEPTH + 1, 1, 128), F32),
            pltpu.VMEM((PLANE, DEPTH + 1, 1, 128), F32),
            pltpu.VMEM((DEPTH, 5, 1, 128), F32),
            pltpu.VMEM((DEPTH, 5, 1, 128), F32),
            pltpu.VMEM((ROWS, ROWS), BF16),
            pltpu.VMEM((ROWS, WIDTH), BF16),
            pltpu.VMEM((1, ROWS), F32),
            pltpu.VMEM((8, ROWS), jnp.int32),
            pltpu.VMEM((4, 2, 4, 2, 8, WIDTH), F32),
            pltpu.VMEM((4, 2, 4, 8, WIDTH), F32),
            pltpu.VMEM((4, 2, 4, 8, WIDTH), F32),
            pltpu.VMEM((15, 2, 8, WIDTH), F32),
            pltpu.VMEM((2, 8, WIDTH), F32),
            pltpu.VMEM((7, 8, WIDTH), F32),
            pltpu.VMEM((3, 1, ROWS), jnp.int32),
            pltpu.VMEM((3, FETCH, WIDTH), BF16),
            pltpu.VMEM((FETCHED, WIDTH), BF16),
            pltpu.VMEM((ROWS, FETCHED), BF16),
            pltpu.VMEM((ROWS, WIDTH), BF16),
            dma((6,)), dma, dma((GROUPS,)), dma, dma, dma, dma,
            dma, dma, dma, dma,
            dma, dma, dma, dma, dma, dma,
            dma, dma((3,)), dma, dma((3,)),
        ],
        compiler_params=pltpu.CompilerParams(
            collective_id=0, has_side_effects=True, vmem_limit_bytes=60 * 2**20
        ),
    )(frames, codebook, linear_map, tile, offset, source)


def shards(frames, codebook, linear_map, code_tile, code_offset, reinit_source):
    commitment, nearest, gradient, fresh, used, over = exchange(
        frames,
        codebook,
        linear_map,
        code_tile.reshape(1, ROWS),
        code_offset.reshape(1, ROWS),
        reinit_source.reshape(1, ROWS),
    )

    def whole_gather():
        here = lax.axis_index("narrow")
        owner = reinit_source >> 10
        row = reinit_source & (ROWS - 1)
        result = jnp.where((owner == here)[:, None], frames[row], codebook)
        for shift in range(1, 4):
            theirs = lax.ppermute(frames, "narrow", [(j, (j - shift) % 4) for j in range(4)])
            result = jnp.where((owner == lax.rem(here + shift, 4))[:, None], theirs[row], result)
        return jnp.where(used.reshape(ROWS, 1) > 0.0, codebook, result)

    new_codebook = lax.cond(over[0, 127] > 0.0, whole_gather, lambda: fresh)
    return commitment.reshape(ROWS), nearest.reshape(ROWS), gradient, new_codebook


def solution(mesh):
    placed = (
        P(("wide", "narrow"), None),
        P(("wide", "narrow"), None),
        P(),
        P(("wide", "narrow"), None),
        P(("wide", "narrow")),
        P(("wide", "narrow")),
    )
    return jax.shard_map(
        shards,
        mesh=mesh,
        in_specs=placed,
        out_specs=(
            P(("wide", "narrow")),
            P(("wide", "narrow")),
            P("wide", None),
            P(("wide", "narrow"), None),
        ),
        check_vma=False,
    )
```

```python
import functools

import jax
import jax.numpy as jnp
from jax import lax
from jax.experimental import pallas as pl
from jax.experimental.pallas import tpu as pltpu
from jax.sharding import PartitionSpec as P

MESH = pl.DeviceIdType.MESH
F32 = jnp.float32
BF16 = jnp.bfloat16

ROWS = 1024
WIDTH = 512
DEVICES = 256
CAP = 8
GROUPS = 8
PER_GROUP = DEVICES // GROUPS
SLOTS = PER_GROUP * CAP
HALF = WIDTH // 2
BLOCK = 2 * CAP
FETCH = 208
SEND_AT = 7
EARLY = 2
PLANE = 32
DEPTH = 8
PLANE_GROUP = PLANE // GROUPS
FETCHED = 640


def coordinates():
    wide = lax.axis_index("wide")
    narrow = lax.axis_index("narrow")
    return (wide // 2) % 4, wide // 16, ((wide // 8) % 2) * 4 + narrow, wide % 2


def device(x, y, z, core):
    return {"wide": ((y * 2 + z // 4) * 4 + x) * 2 + core, "narrow": lax.rem(z, 4)}


def plane_index(step, here, sign):
    x, y, _, core = here
    x2 = lax.rem(x + 4 + sign * lax.rem(step // 2, 4), 4)
    y2 = lax.rem(y + 4 + sign * (step // 8), 4)
    return y2 * 16 + x2 * 2 + lax.rem(core + lax.rem(step, 2), 2)


def column_index(step, here, sign):
    z2 = lax.rem(here[2] + 8 + sign * step, 8)
    return (z2 // 4) * 8, lax.rem(z2, 4)


def iota(shape, dim):
    return lax.broadcasted_iota(jnp.int32, shape, dim)


def nn(a, b):
    return lax.dot_general(a, b, (((1,), (0,)), ((), ())), preferred_element_type=F32)


def nt(a, b):
    return lax.dot_general(a, b, (((1,), (1,)), ((), ())), preferred_element_type=F32)


def tn(a, b):
    return lax.dot_general(a, b, (((0,), (0,)), ((), ())), preferred_element_type=F32)


def one(mask):
    return jnp.where(mask, 1.0, 0.0).astype(BF16)


def remote(src, dst, send, recv, target):
    return pltpu.make_async_remote_copy(
        src_ref=src, dst_ref=dst, send_sem=send, recv_sem=recv, device_id=target, device_id_type=MESH
    )


def drain(ref, sem):
    pltpu.make_async_copy(ref, ref, sem).wait()


def fetch_ranks(source, before):
    owner = source >> 10
    owners = one(owner == iota((16, ROWS), 0))
    counts = nn(owners, before)
    return jnp.sum(owners.astype(F32) * counts, axis=0, keepdims=True).astype(jnp.int32)


def step_kernel(
    frames_in, codebook_in, linear_in, tile_in, offset_in, source_in,
    commit_out, near_out, grad_out, fresh_out, used_out, over_out,
    frames, codebook, linear_map, tile, offset, source, wanted_here,
    outgoing, arrived, labels_out, labels_mid, labels_in, results_out, results_mid, results_pack, results_in,
    before, effective, code_norm, place, total,
    half_in, half_sum, plane_in, plane_sum, column_in,
    asked, rows_out, rows_in, picks, fresh,
    load, data_send, data_recv, column_label_send, column_label_recv, plane_label_send, plane_label_recv,
    plane_result_send, plane_result_recv, column_result_send, column_result_recv,
    half_send, half_recv, plane_send, plane_recv, column_send, column_recv,
    ask_send, ask_recv, row_send, row_recv,
):
    here = coordinates()
    x, y, z, core = here
    narrow = lax.axis_index("narrow")

    loads = [
        pltpu.make_async_copy(src, dst, load.at[i])
        for i, (src, dst) in enumerate(
            (
                (tile_in, tile),
                (offset_in, offset),
                (source_in, source),
                (frames_in, frames),
                (codebook_in, codebook),
                (linear_in, linear_map),
            )
        )
    ]
    for copy in loads:
        copy.start()

    columns = [column_index(step, here, 1) for step in range(DEPTH)]
    plane_here = plane_index(0, here, 1)

    def target(base, step):
        return {"wide": base + columns[step][0], "narrow": columns[step][1]}

    barrier = pltpu.get_barrier_semaphore()
    for step in range(1, DEPTH):
        pl.semaphore_signal(barrier, inc=1, device_id=target(plane_here, step), device_id_type=MESH)

    def greet(step, carry):
        pl.semaphore_signal(
            barrier, inc=1, device_id=target(plane_index(step, here, 1), 0), device_id_type=MESH
        )
        return carry

    lax.fori_loop(1, PLANE, greet, 0)

    before[...] = one(iota((ROWS, ROWS), 0) < iota((ROWS, ROWS), 1))
    for copy in loads[:3]:
        copy.wait()
    named = tile[...]
    wide = named >> 2
    depth = ((wide >> 3) & 1) * 4 + (named & 3)
    step_of = (
        ((depth + 8 - z) & 7)
        + 8 * (((wide & 1) + 2 - core) & 1)
        + 16 * ((((wide >> 1) & 3) + 4 - x) & 3)
        + 64 * (((wide >> 4) + 4 - y) & 3)
    )
    chosen_step = one(step_of == iota((DEVICES, ROWS), 0))
    earlier = nn(chosen_step, before[...])
    rank = jnp.sum(chosen_step.astype(F32) * earlier, axis=0, keepdims=True).astype(jnp.int32)
    place[0:1, :] = step_of
    place[1:2, :] = rank
    place[2:3, :] = step_of * CAP + rank

    label = offset[...] + 1
    at_lane = (step_of >> 3) * CAP + rank == iota((PLANE * CAP, ROWS), 0)
    high = jnp.where(at_lane, (label >> 5).astype(F32), 0.0).astype(BF16)
    low = jnp.where(at_lane, (label & 31).astype(F32), 0.0).astype(BF16)
    chosen_depth = one((step_of & 7) == iota((16, ROWS), 0))
    marks = (32.0 * nt(chosen_depth, high) + nt(chosen_depth, low))[:DEPTH]
    labels_out[:, 0] = marks[:, :128].reshape(DEPTH, 1, 128)
    labels_out[:, 1] = marks[:, 128:].reshape(DEPTH, 1, 128)
    labels_mid[0] = labels_out[0]
    loads[3].wait()

    def dispatch(group):
        slots = iota((SLOTS, ROWS), 0) + group * SLOTS
        picked = nn(one(place[2:3, :] == slots), frames[...])
        left = picked[:, :HALF].reshape(PER_GROUP, 1, CAP, HALF)
        right = picked[:, HALF:].reshape(PER_GROUP, 1, CAP, HALF)
        block = jnp.concatenate([left, right], axis=1).reshape(2 * SLOTS, HALF)
        outgoing[pl.ds(pl.multiple_of(group * 2 * SLOTS, 2 * SLOTS), 2 * SLOTS), :] = block.astype(BF16)

    dispatch(0)

    pl.semaphore_wait(barrier, DEPTH + PLANE - 2)

    for step in range(1, DEPTH):
        remote(
            labels_out.at[step], labels_mid.at[step], column_label_send, column_label_recv,
            target(plane_here, step),
        ).start()
    drain(labels_mid.at[pl.ds(1, DEPTH - 1)], column_label_recv)

    own_label = pltpu.make_async_copy(labels_mid.at[:, 0], labels_in.at[0], plane_label_recv)
    own_label.start()

    def label_plane(step, carry):
        remote(
            labels_mid.at[:, step // 16], labels_in.at[step], plane_label_send, plane_label_recv,
            target(plane_index(step, here, 1), 0),
        ).start()
        return carry

    lax.fori_loop(1, PLANE, label_plane, 0)

    own_data = pltpu.make_async_copy(outgoing.at[pl.ds(0, BLOCK)], arrived.at[pl.ds(0, BLOCK)], data_recv.at[0])
    own_data.start()

    def send(step, first):
        base = plane_index(step, here, 1)
        start = pl.multiple_of(step * (DEPTH * BLOCK), DEPTH * BLOCK)
        for d in range(first, DEPTH):
            rows = pl.ds(start + d * BLOCK, BLOCK)
            remote(
                outgoing.at[rows], arrived.at[rows], data_send, data_recv.at[step // PLANE_GROUP], target(base, d)
            ).start()

    def send_plane(step, carry):
        send(step, 0)
        return carry

    send(0, 1)
    lax.fori_loop(1, PLANE_GROUP, send_plane, 0)

    def dispatch_and_send(group, carry):
        dispatch(group)
        lax.fori_loop(group * PLANE_GROUP, (group + 1) * PLANE_GROUP, send_plane, 0)
        return carry

    lax.fori_loop(1, EARLY, dispatch_and_send, 0)

    drain(labels_in, plane_label_recv)
    row_rank = iota((SLOTS, 128), 0) & (CAP - 1)
    lane = iota((SLOTS, 128), 1)

    plane_step = iota((SLOTS, 128), 0) >> 6

    def codes(group):
        marks = labels_in[pl.ds(group * PLANE_GROUP, PLANE_GROUP)]
        spread = jnp.broadcast_to(marks.reshape(PER_GROUP, 1, 128), (PER_GROUP, CAP, 128)).reshape(SLOTS, 128)
        at = ((plane_step + group * PLANE_GROUP) & 15) * CAP + row_rank
        mark = jnp.sum(jnp.where(lane == at, spread, 0.0), axis=1, keepdims=True)
        return (mark.astype(jnp.int32) - 1) == iota((SLOTS, ROWS), 1)

    def count(group, used):
        return used + jnp.sum(jnp.where(codes(group), 1.0, 0.0), axis=0, keepdims=True)

    used = lax.fori_loop(0, GROUPS, count, jnp.zeros((1, ROWS), F32))
    used_out[...] = used
    wanted = jnp.where(used > 0.0, 8 * ROWS, source[...])
    wanted_here[...] = wanted
    for j in range(3):
        peer = {"narrow": lax.rem(narrow + j + 1, 4)}
        remote(wanted_here, asked.at[j], ask_send, ask_recv.at[j], peer).start()
    lax.fori_loop(EARLY, GROUPS, dispatch_and_send, 0)
    fetch_rank = fetch_ranks(wanted, before[...])
    far = ((wanted >> 10) != narrow) & (used == 0.0)
    over = jnp.max(jnp.where(far & (fetch_rank >= FETCH), 1.0, 0.0), axis=1, keepdims=True)
    results_out[:, DEPTH] = jnp.broadcast_to(over.reshape(1, 1, 1), (PLANE, 1, 128))

    for copy in loads[4:]:
        copy.wait()
    eff = nn(codebook[...], linear_map[...]).astype(BF16)
    effective[...] = eff
    eff_f = eff.astype(F32)
    norms = jnp.sum(eff_f * eff_f, axis=1, keepdims=True)
    code_norm[...] = jnp.transpose(jnp.broadcast_to(norms, (ROWS, 128)))[0:1, :]
    total[...] = jnp.zeros_like(total)

    for j in range(3):
        drain(asked.at[j], ask_recv.at[j])
        theirs = asked[j]
        order = fetch_ranks(theirs, before[...])
        mine = ((theirs >> 10) == narrow) & (order == iota((FETCH, ROWS), 0))
        index = jnp.sum(jnp.where(mine, (theirs & 1023).astype(F32), 0.0), axis=1, keepdims=True)
        rows = one(index.astype(jnp.int32) == iota((FETCH, ROWS), 1))
        rows_out[j] = nn(rows, frames[...]).astype(BF16)

    mine = ((wanted >> 10) == narrow) & ((wanted & 1023) == iota((ROWS, ROWS), 0))
    used_column = jnp.transpose(jnp.broadcast_to(used, (128, ROWS)))[:, 0:1]
    fresh[...] = jnp.where(used_column > 0.0, codebook[...].astype(F32), tn(one(mine), frames[...])).astype(BF16)
    asked_for = [
        jnp.where(((wanted >> 10) == lax.rem(narrow + j + 1, 4)) & (fetch_rank == iota((FETCH, ROWS), 0)), 1.0, 0.0)
        for j in range(3)
    ]
    spare = FETCHED - 3 * FETCH
    picks[...] = jnp.transpose(jnp.concatenate(asked_for + [jnp.zeros((spare, ROWS), F32)], axis=0)).astype(BF16)
    rows_in[pl.ds(3 * FETCH, spare), :] = jnp.zeros((spare, WIDTH), BF16)

    def work(group, carry):
        rows = pl.ds(pl.multiple_of(group * 2 * SLOTS, 2 * SLOTS), 2 * SLOTS)
        drain(arrived.at[rows], data_recv.at[group])

        @pl.when(group == SEND_AT)
        def _():
            for j in range(3):
                peer = {"narrow": lax.rem(narrow + 3 - j, 4)}
                remote(
                    rows_out.at[j], rows_in.at[pl.ds(j * FETCH, FETCH)], row_send, row_recv.at[j], peer
                ).start()

        parts = arrived[rows, :].astype(F32).reshape(PER_GROUP, 2, CAP, HALF)
        taken_f = jnp.concatenate(
            [parts[:, 0].reshape(SLOTS, HALF), parts[:, 1].reshape(SLOTS, HALF)], axis=1
        )
        taken = taken_f.astype(BF16)
        chosen_mask = codes(group)
        selector = one(chosen_mask)
        quantized = nn(selector, effective[...])
        chosen = nn(selector, codebook[...]).astype(BF16)
        gap = quantized - taken_f
        commitment = jnp.sum(gap * gap, axis=1, keepdims=True) * (1.0 / WIDTH)
        cross = nt(taken, effective[...])
        least = jnp.min(code_norm[...] - 2.0 * cross, axis=1, keepdims=True)
        nearest = (jnp.sum(taken_f * taken_f, axis=1, keepdims=True) + least) * (1.0 / WIDTH)
        total[...] += tn(chosen, gap.astype(BF16)).reshape(total.shape)
        at = ((plane_step + group * PLANE_GROUP) & 7) * (2 * CAP) + row_rank
        back = jnp.where(lane == at, commitment, 0.0) + jnp.where(lane == at + CAP, nearest, 0.0)
        back = jnp.sum(back.reshape(PER_GROUP, CAP, 128), axis=1, keepdims=True)
        results_out[pl.ds(group * PLANE_GROUP, PLANE_GROUP), pl.ds(0, DEPTH)] = back.reshape(PLANE_GROUP, DEPTH, 1, 128)

        def give(step):
            remote(
                results_out.at[step], results_mid.at[step], plane_result_send, plane_result_recv,
                target(plane_index(step, here, -1), 0),
            ).start()

        @pl.when(group > 0)
        def _():
            give(group * PLANE_GROUP)

        @pl.when(group == 0)
        def _():
            pltpu.make_async_copy(results_out.at[0], results_mid.at[0], plane_result_recv).start()

        for step in range(1, PLANE_GROUP):
            give(group * PLANE_GROUP + step)
        return carry

    lax.fori_loop(0, GROUPS, work, 0)

    to_pair = remote(total.at[:, :, :, 1 - core], half_in, half_send, half_recv, device(x, y, z, 1 - core))
    to_pair.start()

    to_pair.wait()
    half_sum[...] = total[:, :, :, core] + half_in[...]
    for step in range(1, 16):
        x2 = lax.rem(x + step % 4, 4)
        y2 = lax.rem(y + step // 4, 4)
        remote(
            half_sum.at[y2, :, x2], plane_in.at[step - 1], plane_send, plane_recv, device(x2, y2, z, core)
        ).start()

    drain(results_mid, plane_result_recv)
    for block in range(4):
        results_pack[:, block] = jnp.sum(results_mid[pl.ds(block * 8, 8), pl.ds(0, DEPTH)], axis=0)
    results_pack[:, 4] = jnp.broadcast_to(jnp.max(results_mid[:, DEPTH], axis=0, keepdims=True), (DEPTH, 1, 128))
    results_in[0] = results_pack[0]
    for step in range(1, DEPTH):
        offset_wide, narrow_back = column_index(step, here, -1)
        remote(
            results_pack.at[step], results_in.at[step], column_result_send, column_result_recv,
            {"wide": plane_here + offset_wide, "narrow": narrow_back},
        ).start()

    drain(plane_in, plane_recv)
    plane_sum[...] = half_sum[y, :, x] + jnp.sum(plane_in[...], axis=0)
    for step in range(1, 8):
        z2 = lax.rem(z + step, 8)
        remote(
            plane_sum.at[z2 // 4], column_in.at[step - 1], column_send, column_recv, device(x, y, z2, core)
        ).start()

    drain(results_in.at[pl.ds(1, DEPTH - 1)], column_result_recv)
    over_out[0, 0] = jnp.max(results_in[:, 4]).astype(jnp.int32)
    returned = results_in[:, pl.ds(0, 4)].reshape(PLANE, 128)
    step_of = place[0:1, :]
    steps = one((step_of & 7) * 4 + (step_of >> 6) == iota((PLANE, ROWS), 0))
    first = returned.astype(BF16)
    rest = returned - first.astype(F32)
    second = rest.astype(BF16)
    third = (rest - second.astype(F32)).astype(BF16)
    home = tn(first, steps) + tn(second, steps) + tn(third, steps)
    at = ((step_of >> 3) & 7) * (2 * CAP) + place[1:2, :]
    commit_out[...] = jnp.sum(jnp.where(at == iota((128, ROWS), 0), home, 0.0), axis=0, keepdims=True)
    near_out[...] = jnp.sum(jnp.where(at + CAP == iota((128, ROWS), 0), home, 0.0), axis=0, keepdims=True)

    for j in range(3):
        drain(rows_in.at[pl.ds(j * FETCH, FETCH)], row_recv.at[j])
    fresh_out[...] = (fresh[...].astype(F32) + nn(picks[...], rows_in[...])).astype(BF16)

    drain(column_in, column_recv)
    grad_out[...] = (plane_sum[z // 4] + jnp.sum(column_in[...], axis=0)) * (2.0 / 512.0)

    sent = pl.ds(BLOCK, (DEVICES - 1) * BLOCK)
    drain(outgoing.at[sent], data_send)
    drain(labels_mid.at[pl.ds(1, DEPTH - 1)], column_label_send)
    drain(labels_in.at[pl.ds(1, PLANE - 1)], plane_label_send)
    drain(results_mid.at[pl.ds(1, PLANE - 1)], plane_result_send)
    drain(results_in.at[pl.ds(1, DEPTH - 1)], column_result_send)
    drain(plane_in, plane_send)
    drain(column_in, column_send)
    drain(asked, ask_send)
    drain(rows_out, row_send)


def exchange(frames, codebook, linear_map, tile, offset, source):
    vmem = pl.BlockSpec(memory_space=pltpu.VMEM)
    dma = pltpu.SemaphoreType.DMA
    return pl.pallas_call(
        step_kernel,
        out_shape=[
            jax.ShapeDtypeStruct((1, ROWS), F32),
            jax.ShapeDtypeStruct((1, ROWS), F32),
            jax.ShapeDtypeStruct((CAP, WIDTH), F32),
            jax.ShapeDtypeStruct((ROWS, WIDTH), BF16),
            jax.ShapeDtypeStruct((1, ROWS), F32),
            jax.ShapeDtypeStruct((1, 1), jnp.int32),
        ],
        in_specs=[pl.BlockSpec(memory_space=pl.ANY)] * 6,
        out_specs=[vmem] * 5 + [pl.BlockSpec(memory_space=pltpu.SMEM)],
        scratch_shapes=[
            pltpu.VMEM((ROWS, WIDTH), BF16),
            pltpu.VMEM((ROWS, WIDTH), BF16),
            pltpu.VMEM((WIDTH, WIDTH), BF16),
            pltpu.VMEM((1, ROWS), jnp.int32),
            pltpu.VMEM((1, ROWS), jnp.int32),
            pltpu.VMEM((1, ROWS), jnp.int32),
            pltpu.VMEM((1, ROWS), jnp.int32),
            pltpu.VMEM((DEVICES * BLOCK, HALF), BF16),
            pltpu.VMEM((DEVICES * BLOCK, HALF), BF16),
            pltpu.VMEM((DEPTH, 2, 1, 128), F32),
            pltpu.VMEM((DEPTH, 2, 1, 128), F32),
            pltpu.VMEM((PLANE, DEPTH, 1, 128), F32),
            pltpu.VMEM((PLANE, DEPTH + 1, 1, 128), F32),
            pltpu.VMEM((PLANE, DEPTH + 1, 1, 128), F32),
            pltpu.VMEM((DEPTH, 5, 1, 128), F32),
            pltpu.VMEM((DEPTH, 5, 1, 128), F32),
            pltpu.VMEM((ROWS, ROWS), BF16),
            pltpu.VMEM((ROWS, WIDTH), BF16),
            pltpu.VMEM((1, ROWS), F32),
            pltpu.VMEM((8, ROWS), jnp.int32),
            pltpu.VMEM((4, 2, 4, 2, 8, WIDTH), F32),
            pltpu.VMEM((4, 2, 4, 8, WIDTH), F32),
            pltpu.VMEM((4, 2, 4, 8, WIDTH), F32),
            pltpu.VMEM((15, 2, 8, WIDTH), F32),
            pltpu.VMEM((2, 8, WIDTH), F32),
            pltpu.VMEM((7, 8, WIDTH), F32),
            pltpu.VMEM((3, 1, ROWS), jnp.int32),
            pltpu.VMEM((3, FETCH, WIDTH), BF16),
            pltpu.VMEM((FETCHED, WIDTH), BF16),
            pltpu.VMEM((ROWS, FETCHED), BF16),
            pltpu.VMEM((ROWS, WIDTH), BF16),
            dma((6,)), dma, dma((GROUPS,)), dma, dma, dma, dma,
            dma, dma, dma, dma,
            dma, dma, dma, dma, dma, dma,
            dma, dma((3,)), dma, dma((3,)),
        ],
        compiler_params=pltpu.CompilerParams(
            collective_id=0, has_side_effects=True, vmem_limit_bytes=60 * 2**20
        ),
    )(frames, codebook, linear_map, tile, offset, source)


def publish_kernel(*refs):
    sources, results, sems = refs[:4], refs[4:8], refs[8]
    copies = [pltpu.make_async_copy(src, dst, sems.at[i]) for i, (src, dst) in enumerate(zip(sources, results))]
    for copy in copies:
        copy.start()
    for copy in copies:
        copy.wait()


def publish(*arrays):
    anywhere = pl.BlockSpec(memory_space=pl.ANY)
    return pl.pallas_call(
        publish_kernel,
        out_shape=[jax.ShapeDtypeStruct(a.shape, a.dtype) for a in arrays],
        in_specs=[anywhere] * 4,
        out_specs=[anywhere] * 4,
        scratch_shapes=[pltpu.SemaphoreType.DMA((4,))],
    )(*arrays)


def shards(frames, codebook, linear_map, code_tile, code_offset, reinit_source):
    commitment, nearest, gradient, fresh, used, over = exchange(
        frames,
        codebook,
        linear_map,
        code_tile.reshape(1, ROWS),
        code_offset.reshape(1, ROWS),
        reinit_source.reshape(1, ROWS),
    )

    def whole_gather():
        here = lax.axis_index("narrow")
        owner = reinit_source >> 10
        row = reinit_source & (ROWS - 1)
        result = jnp.where((owner == here)[:, None], frames[row], codebook)
        for shift in range(1, 4):
            theirs = lax.ppermute(frames, "narrow", [(j, (j - shift) % 4) for j in range(4)])
            result = jnp.where((owner == lax.rem(here + shift, 4))[:, None], theirs[row], result)
        return jnp.where(used.reshape(ROWS, 1) > 0.0, codebook, result)

    new_codebook = lax.cond(over[0, 0] > 0, whole_gather, lambda: fresh)
    commitment, nearest, gradient, new_codebook = publish(commitment, nearest, gradient, new_codebook)
    return commitment.reshape(ROWS), nearest.reshape(ROWS), gradient, new_codebook


def solution(mesh):
    placed = (
        P(("wide", "narrow"), None),
        P(("wide", "narrow"), None),
        P(),
        P(("wide", "narrow"), None),
        P(("wide", "narrow")),
        P(("wide", "narrow")),
    )
    return jax.shard_map(
        shards,
        mesh=mesh,
        in_specs=placed,
        out_specs=(
            P(("wide", "narrow")),
            P(("wide", "narrow")),
            P("wide", None),
            P(("wide", "narrow"), None),
        ),
        check_vma=False,
    )
```

```python
import functools

import jax
import jax.numpy as jnp
from jax import lax
from jax.experimental import pallas as pl
from jax.experimental.pallas import tpu as pltpu
from jax.sharding import PartitionSpec as P

MESH = pl.DeviceIdType.MESH
F32 = jnp.float32
BF16 = jnp.bfloat16

ROWS = 1024
WIDTH = 512
DEVICES = 256
CAP = 8
GROUPS = 8
PER_GROUP = DEVICES // GROUPS
SLOTS = PER_GROUP * CAP
HALF = WIDTH // 2
BLOCK = 2 * CAP
FETCH = 192
SEND_AT = (6, 6, 8)
EARLY = 2
PLANE = 32
DEPTH = 8
PLANE_GROUP = PLANE // GROUPS
FETCHED = 640


def coordinates():
    wide = lax.axis_index("wide")
    narrow = lax.axis_index("narrow")
    return (wide // 2) % 4, wide // 16, ((wide // 8) % 2) * 4 + narrow, wide % 2


def device(x, y, z, core):
    return {"wide": ((y * 2 + z // 4) * 4 + x) * 2 + core, "narrow": lax.rem(z, 4)}


def plane_index(step, here, sign):
    x, y, _, core = here
    x2 = lax.rem(x + 4 + sign * lax.rem(step // 2, 4), 4)
    y2 = lax.rem(y + 4 + sign * (step // 8), 4)
    return y2 * 16 + x2 * 2 + lax.rem(core + lax.rem(step, 2), 2)


def column_index(step, here, sign):
    z2 = lax.rem(here[2] + 8 + sign * step, 8)
    return (z2 // 4) * 8, lax.rem(z2, 4)


def iota(shape, dim):
    return lax.broadcasted_iota(jnp.int32, shape, dim)


def nn(a, b):
    return lax.dot_general(a, b, (((1,), (0,)), ((), ())), preferred_element_type=F32)


def nt(a, b):
    return lax.dot_general(a, b, (((1,), (1,)), ((), ())), preferred_element_type=F32)


def tn(a, b):
    return lax.dot_general(a, b, (((0,), (0,)), ((), ())), preferred_element_type=F32)


def one(mask):
    return jnp.where(mask, 1.0, 0.0).astype(BF16)


def remote(src, dst, send, recv, target):
    return pltpu.make_async_remote_copy(
        src_ref=src, dst_ref=dst, send_sem=send, recv_sem=recv, device_id=target, device_id_type=MESH
    )


def drain(ref, sem):
    pltpu.make_async_copy(ref, ref, sem).wait()


def fetch_ranks(source, before):
    owner = source >> 10
    owners = one(owner == iota((16, ROWS), 0))
    counts = nn(owners, before)
    return jnp.sum(owners.astype(F32) * counts, axis=0, keepdims=True).astype(jnp.int32)


def step_kernel(
    frames_in, codebook_in, linear_in, tile_in, offset_in, source_in,
    commit_out, near_out, grad_out, fresh_out, used_out, over_out,
    frames, codebook, linear_map, tile, offset, source, wanted_here,
    outgoing, arrived, labels_out, labels_mid, labels_in, results_out, results_mid, results_pack, results_in,
    before, effective, code_norm, place, total,
    half_in, half_sum, plane_in, plane_sum, column_in,
    asked, rows_out, rows_in, picks, fresh,
    load, data_send, data_recv, column_label_send, column_label_recv, plane_label_send, plane_label_recv,
    plane_result_send, plane_result_recv, column_result_send, column_result_recv,
    half_send, half_recv, plane_send, plane_recv, column_send, column_recv,
    ask_send, ask_recv, row_send, row_recv,
):
    here = coordinates()
    x, y, z, core = here
    narrow = lax.axis_index("narrow")

    loads = [
        pltpu.make_async_copy(src, dst, load.at[i])
        for i, (src, dst) in enumerate(
            (
                (tile_in, tile),
                (offset_in, offset),
                (source_in, source),
                (frames_in, frames),
                (codebook_in, codebook),
                (linear_in, linear_map),
            )
        )
    ]
    for copy in loads:
        copy.start()

    columns = [column_index(step, here, 1) for step in range(DEPTH)]
    plane_here = plane_index(0, here, 1)

    def target(base, step):
        return {"wide": base + columns[step][0], "narrow": columns[step][1]}

    barrier = pltpu.get_barrier_semaphore()
    for step in range(1, DEPTH):
        pl.semaphore_signal(barrier, inc=1, device_id=target(plane_here, step), device_id_type=MESH)

    def greet(step, carry):
        pl.semaphore_signal(
            barrier, inc=1, device_id=target(plane_index(step, here, 1), 0), device_id_type=MESH
        )
        return carry

    lax.fori_loop(1, PLANE, greet, 0)

    before[...] = one(iota((ROWS, ROWS), 0) < iota((ROWS, ROWS), 1))
    for copy in loads[:3]:
        copy.wait()
    named = tile[...]
    wide = named >> 2
    depth = ((wide >> 3) & 1) * 4 + (named & 3)
    step_of = (
        ((depth + 8 - z) & 7)
        + 8 * (((wide & 1) + 2 - core) & 1)
        + 16 * ((((wide >> 1) & 3) + 4 - x) & 3)
        + 64 * (((wide >> 4) + 4 - y) & 3)
    )
    chosen_step = one(step_of == iota((DEVICES, ROWS), 0))
    earlier = nn(chosen_step, before[...])
    rank = jnp.sum(chosen_step.astype(F32) * earlier, axis=0, keepdims=True).astype(jnp.int32)
    place[0:1, :] = step_of
    place[1:2, :] = rank
    place[2:3, :] = step_of * CAP + rank

    label = offset[...] + 1
    at_lane = (step_of >> 3) * CAP + rank == iota((PLANE * CAP, ROWS), 0)
    high = jnp.where(at_lane, (label >> 5).astype(F32), 0.0).astype(BF16)
    low = jnp.where(at_lane, (label & 31).astype(F32), 0.0).astype(BF16)
    chosen_depth = one((step_of & 7) == iota((16, ROWS), 0))
    marks = (32.0 * nt(chosen_depth, high) + nt(chosen_depth, low))[:DEPTH]
    labels_out[:, 0] = marks[:, :128].reshape(DEPTH, 1, 128)
    labels_out[:, 1] = marks[:, 128:].reshape(DEPTH, 1, 128)
    labels_mid[0] = labels_out[0]

    def dispatch(group):
        slots = iota((SLOTS, ROWS), 0) + group * SLOTS
        picked = nn(one(place[2:3, :] == slots), frames[...])
        left = picked[:, :HALF].reshape(PER_GROUP, 1, CAP, HALF)
        right = picked[:, HALF:].reshape(PER_GROUP, 1, CAP, HALF)
        block = jnp.concatenate([left, right], axis=1).reshape(2 * SLOTS, HALF)
        outgoing[pl.ds(pl.multiple_of(group * 2 * SLOTS, 2 * SLOTS), 2 * SLOTS), :] = block.astype(BF16)

    pl.semaphore_wait(barrier, DEPTH + PLANE - 2)

    for step in range(1, DEPTH):
        remote(
            labels_out.at[step], labels_mid.at[step], column_label_send, column_label_recv,
            target(plane_here, step),
        ).start()
    loads[3].wait()
    dispatch(0)
    drain(labels_mid.at[pl.ds(1, DEPTH - 1)], column_label_recv)

    own_label = pltpu.make_async_copy(labels_mid.at[:, 0], labels_in.at[0], plane_label_recv)
    own_label.start()

    def label_plane(step, carry):
        remote(
            labels_mid.at[:, step // 16], labels_in.at[step], plane_label_send, plane_label_recv,
            target(plane_index(step, here, 1), 0),
        ).start()
        return carry

    lax.fori_loop(1, PLANE, label_plane, 0)

    own_data = pltpu.make_async_copy(outgoing.at[pl.ds(0, BLOCK)], arrived.at[pl.ds(0, BLOCK)], data_recv.at[0])
    own_data.start()

    def send(step, first):
        base = plane_index(step, here, 1)
        start = pl.multiple_of(step * (DEPTH * BLOCK), DEPTH * BLOCK)
        for d in range(first, DEPTH):
            rows = pl.ds(start + d * BLOCK, BLOCK)
            remote(
                outgoing.at[rows], arrived.at[rows], data_send, data_recv.at[step // PLANE_GROUP], target(base, d)
            ).start()

    def send_plane(step, carry):
        send(step, 0)
        return carry

    send(0, 1)
    lax.fori_loop(1, PLANE_GROUP, send_plane, 0)

    def dispatch_and_send(group, carry):
        dispatch(group)
        lax.fori_loop(group * PLANE_GROUP, (group + 1) * PLANE_GROUP, send_plane, 0)
        return carry

    lax.fori_loop(1, EARLY, dispatch_and_send, 0)

    drain(labels_in, plane_label_recv)
    row_rank = iota((SLOTS, 128), 0) & (CAP - 1)
    lane = iota((SLOTS, 128), 1)

    plane_step = iota((SLOTS, 128), 0) >> 6

    def codes(group):
        marks = labels_in[pl.ds(group * PLANE_GROUP, PLANE_GROUP)]
        spread = jnp.broadcast_to(marks.reshape(PER_GROUP, 1, 128), (PER_GROUP, CAP, 128)).reshape(SLOTS, 128)
        at = ((plane_step + group * PLANE_GROUP) & 15) * CAP + row_rank
        mark = jnp.sum(jnp.where(lane == at, spread, 0.0), axis=1, keepdims=True)
        return (mark.astype(jnp.int32) - 1) == iota((SLOTS, ROWS), 1)

    def count(group, used):
        return used + jnp.sum(jnp.where(codes(group), 1.0, 0.0), axis=0, keepdims=True)

    used = lax.fori_loop(0, GROUPS, count, jnp.zeros((1, ROWS), F32))
    used_out[...] = used
    wanted = jnp.where(used > 0.0, 8 * ROWS, source[...])
    wanted_here[...] = wanted
    for j in range(3):
        peer = {"narrow": lax.rem(narrow + j + 1, 4)}
        remote(wanted_here, asked.at[j], ask_send, ask_recv.at[j], peer).start()
    lax.fori_loop(EARLY, GROUPS, dispatch_and_send, 0)
    fetch_rank = fetch_ranks(wanted, before[...])
    far = ((wanted >> 10) != narrow) & (used == 0.0)
    over = jnp.max(jnp.where(far & (fetch_rank >= FETCH), 1.0, 0.0), axis=1, keepdims=True)
    results_out[:, DEPTH] = jnp.broadcast_to(over.reshape(1, 1, 1), (PLANE, 1, 128))

    for copy in loads[4:]:
        copy.wait()
    eff = nn(codebook[...], linear_map[...]).astype(BF16)
    effective[...] = eff
    eff_f = eff.astype(F32)
    norms = jnp.sum(eff_f * eff_f, axis=1, keepdims=True)
    code_norm[...] = jnp.transpose(jnp.broadcast_to(norms, (ROWS, 128)))[0:1, :]
    total[...] = jnp.zeros_like(total)

    for j in range(3):
        drain(asked.at[j], ask_recv.at[j])
        theirs = asked[j]
        order = fetch_ranks(theirs, before[...])
        mine = ((theirs >> 10) == narrow) & (order == iota((FETCH, ROWS), 0))
        index = jnp.sum(jnp.where(mine, (theirs & 1023).astype(F32), 0.0), axis=1, keepdims=True)
        rows = one(index.astype(jnp.int32) == iota((FETCH, ROWS), 1))
        rows_out[j] = nn(rows, frames[...]).astype(BF16)

    mine = ((wanted >> 10) == narrow) & ((wanted & 1023) == iota((ROWS, ROWS), 0))
    used_column = jnp.transpose(jnp.broadcast_to(used, (128, ROWS)))[:, 0:1]
    fresh[...] = jnp.where(used_column > 0.0, codebook[...].astype(F32), tn(one(mine), frames[...])).astype(BF16)
    asked_for = [
        jnp.where(((wanted >> 10) == lax.rem(narrow + j + 1, 4)) & (fetch_rank == iota((FETCH, ROWS), 0)), 1.0, 0.0)
        for j in range(3)
    ]
    spare = FETCHED - 3 * FETCH
    picks[...] = jnp.transpose(jnp.concatenate(asked_for + [jnp.zeros((spare, ROWS), F32)], axis=0)).astype(BF16)
    rows_in[pl.ds(3 * FETCH, spare), :] = jnp.zeros((spare, WIDTH), BF16)

    def respond(j):
        peer = {"narrow": lax.rem(narrow + 3 - j, 4)}
        remote(
            rows_out.at[j], rows_in.at[pl.ds(j * FETCH, FETCH)], row_send, row_recv.at[j], peer
        ).start()

    def work(group, carry):
        rows = pl.ds(pl.multiple_of(group * 2 * SLOTS, 2 * SLOTS), 2 * SLOTS)
        drain(arrived.at[rows], data_recv.at[group])

        for j in range(3):
            if SEND_AT[j] < GROUPS:
                pl.when(group == SEND_AT[j])(functools.partial(respond, j))

        parts = arrived[rows, :].astype(F32).reshape(PER_GROUP, 2, CAP, HALF)
        taken_f = jnp.concatenate(
            [parts[:, 0].reshape(SLOTS, HALF), parts[:, 1].reshape(SLOTS, HALF)], axis=1
        )
        taken = taken_f.astype(BF16)
        chosen_mask = codes(group)
        selector = one(chosen_mask)
        quantized = nn(selector, effective[...])
        chosen = nn(selector, codebook[...]).astype(BF16)
        gap = quantized - taken_f
        commitment = jnp.sum(gap * gap, axis=1, keepdims=True) * (1.0 / WIDTH)
        cross = nt(taken, effective[...])
        least = jnp.min(code_norm[...] - 2.0 * cross, axis=1, keepdims=True)
        nearest = (jnp.sum(taken_f * taken_f, axis=1, keepdims=True) + least) * (1.0 / WIDTH)
        total[...] += tn(chosen, gap.astype(BF16)).reshape(total.shape)
        at = ((plane_step + group * PLANE_GROUP) & 7) * (2 * CAP) + row_rank
        back = jnp.where(lane == at, commitment, 0.0) + jnp.where(lane == at + CAP, nearest, 0.0)
        back = jnp.sum(back.reshape(PER_GROUP, CAP, 128), axis=1, keepdims=True)
        results_out[pl.ds(group * PLANE_GROUP, PLANE_GROUP), pl.ds(0, DEPTH)] = back.reshape(PLANE_GROUP, DEPTH, 1, 128)

        def give(step):
            remote(
                results_out.at[step], results_mid.at[step], plane_result_send, plane_result_recv,
                target(plane_index(step, here, -1), 0),
            ).start()

        @pl.when(group > 0)
        def _():
            give(group * PLANE_GROUP)

        @pl.when(group == 0)
        def _():
            pltpu.make_async_copy(results_out.at[0], results_mid.at[0], plane_result_recv).start()

        for step in range(1, PLANE_GROUP):
            give(group * PLANE_GROUP + step)
        return carry

    lax.fori_loop(0, GROUPS, work, 0)

    to_pair = remote(total.at[:, :, :, 1 - core], half_in, half_send, half_recv, device(x, y, z, 1 - core))
    to_pair.start()

    to_pair.wait()
    half_sum[...] = total[:, :, :, core] + half_in[...]
    for step in range(1, 16):
        x2 = lax.rem(x + step % 4, 4)
        y2 = lax.rem(y + step // 4, 4)
        remote(
            half_sum.at[y2, :, x2], plane_in.at[step - 1], plane_send, plane_recv, device(x2, y2, z, core)
        ).start()

    drain(results_mid, plane_result_recv)
    for block in range(4):
        results_pack[:, block] = jnp.sum(results_mid[pl.ds(block * 8, 8), pl.ds(0, DEPTH)], axis=0)
    results_pack[:, 4] = jnp.broadcast_to(jnp.max(results_mid[:, DEPTH], axis=0, keepdims=True), (DEPTH, 1, 128))
    results_in[0] = results_pack[0]
    for step in range(1, DEPTH):
        offset_wide, narrow_back = column_index(step, here, -1)
        remote(
            results_pack.at[step], results_in.at[step], column_result_send, column_result_recv,
            {"wide": plane_here + offset_wide, "narrow": narrow_back},
        ).start()
    for j in range(3):
        if SEND_AT[j] == GROUPS:
            respond(j)

    drain(plane_in, plane_recv)
    plane_sum[...] = half_sum[y, :, x] + jnp.sum(plane_in[...], axis=0)
    for step in range(1, 8):
        z2 = lax.rem(z + step, 8)
        remote(
            plane_sum.at[z2 // 4], column_in.at[step - 1], column_send, column_recv, device(x, y, z2, core)
        ).start()

    drain(results_in.at[pl.ds(1, DEPTH - 1)], column_result_recv)
    over_out[0, 0] = jnp.max(results_in[:, 4]).astype(jnp.int32)
    returned = results_in[:, pl.ds(0, 4)].reshape(PLANE, 128)
    step_of = place[0:1, :]
    steps = one((step_of & 7) * 4 + (step_of >> 6) == iota((PLANE, ROWS), 0))
    first = returned.astype(BF16)
    rest = returned - first.astype(F32)
    second = rest.astype(BF16)
    third = (rest - second.astype(F32)).astype(BF16)
    home = tn(first, steps) + tn(second, steps) + tn(third, steps)
    at = ((step_of >> 3) & 7) * (2 * CAP) + place[1:2, :]
    commit_out[...] = jnp.sum(jnp.where(at == iota((128, ROWS), 0), home, 0.0), axis=0, keepdims=True)
    near_out[...] = jnp.sum(jnp.where(at + CAP == iota((128, ROWS), 0), home, 0.0), axis=0, keepdims=True)

    for j in range(3):
        drain(rows_in.at[pl.ds(j * FETCH, FETCH)], row_recv.at[j])
    fresh_out[...] = (fresh[...].astype(F32) + nn(picks[...], rows_in[...])).astype(BF16)

    drain(column_in, column_recv)
    grad_out[...] = (plane_sum[z // 4] + jnp.sum(column_in[...], axis=0)) * (2.0 / 512.0)

    sent = pl.ds(BLOCK, (DEVICES - 1) * BLOCK)
    drain(outgoing.at[sent], data_send)
    drain(labels_mid.at[pl.ds(1, DEPTH - 1)], column_label_send)
    drain(labels_in.at[pl.ds(1, PLANE - 1)], plane_label_send)
    drain(results_mid.at[pl.ds(1, PLANE - 1)], plane_result_send)
    drain(results_in.at[pl.ds(1, DEPTH - 1)], column_result_send)
    drain(plane_in, plane_send)
    drain(column_in, column_send)
    drain(asked, ask_send)
    drain(rows_out, row_send)


def exchange(frames, codebook, linear_map, tile, offset, source):
    vmem = pl.BlockSpec(memory_space=pltpu.VMEM)
    dma = pltpu.SemaphoreType.DMA
    return pl.pallas_call(
        step_kernel,
        out_shape=[
            jax.ShapeDtypeStruct((1, ROWS), F32),
            jax.ShapeDtypeStruct((1, ROWS), F32),
            jax.ShapeDtypeStruct((CAP, WIDTH), F32),
            jax.ShapeDtypeStruct((ROWS, WIDTH), BF16),
            jax.ShapeDtypeStruct((1, ROWS), F32),
            jax.ShapeDtypeStruct((1, 1), jnp.int32),
        ],
        in_specs=[pl.BlockSpec(memory_space=pl.ANY)] * 6,
        out_specs=[vmem] * 5 + [pl.BlockSpec(memory_space=pltpu.SMEM)],
        scratch_shapes=[
            pltpu.VMEM((ROWS, WIDTH), BF16),
            pltpu.VMEM((ROWS, WIDTH), BF16),
            pltpu.VMEM((WIDTH, WIDTH), BF16),
            pltpu.VMEM((1, ROWS), jnp.int32),
            pltpu.VMEM((1, ROWS), jnp.int32),
            pltpu.VMEM((1, ROWS), jnp.int32),
            pltpu.VMEM((1, ROWS), jnp.int32),
            pltpu.VMEM((DEVICES * BLOCK, HALF), BF16),
            pltpu.VMEM((DEVICES * BLOCK, HALF), BF16),
            pltpu.VMEM((DEPTH, 2, 1, 128), F32),
            pltpu.VMEM((DEPTH, 2, 1, 128), F32),
            pltpu.VMEM((PLANE, DEPTH, 1, 128), F32),
            pltpu.VMEM((PLANE, DEPTH + 1, 1, 128), F32),
            pltpu.VMEM((PLANE, DEPTH + 1, 1, 128), F32),
            pltpu.VMEM((DEPTH, 5, 1, 128), F32),
            pltpu.VMEM((DEPTH, 5, 1, 128), F32),
            pltpu.VMEM((ROWS, ROWS), BF16),
            pltpu.VMEM((ROWS, WIDTH), BF16),
            pltpu.VMEM((1, ROWS), F32),
            pltpu.VMEM((8, ROWS), jnp.int32),
            pltpu.VMEM((4, 2, 4, 2, 8, WIDTH), F32),
            pltpu.VMEM((4, 2, 4, 8, WIDTH), F32),
            pltpu.VMEM((4, 2, 4, 8, WIDTH), F32),
            pltpu.VMEM((15, 2, 8, WIDTH), F32),
            pltpu.VMEM((2, 8, WIDTH), F32),
            pltpu.VMEM((7, 8, WIDTH), F32),
            pltpu.VMEM((3, 1, ROWS), jnp.int32),
            pltpu.VMEM((3, FETCH, WIDTH), BF16),
            pltpu.VMEM((FETCHED, WIDTH), BF16),
            pltpu.VMEM((ROWS, FETCHED), BF16),
            pltpu.VMEM((ROWS, WIDTH), BF16),
            dma((6,)), dma, dma((GROUPS,)), dma, dma, dma, dma,
            dma, dma, dma, dma,
            dma, dma, dma, dma, dma, dma,
            dma, dma((3,)), dma, dma((3,)),
        ],
        compiler_params=pltpu.CompilerParams(
            collective_id=0, has_side_effects=True, vmem_limit_bytes=60 * 2**20
        ),
    )(frames, codebook, linear_map, tile, offset, source)


def publish_kernel(*refs):
    sources, results, sems = refs[:4], refs[4:8], refs[8]
    copies = [pltpu.make_async_copy(src, dst, sems.at[i]) for i, (src, dst) in enumerate(zip(sources, results))]
    for copy in copies:
        copy.start()
    for copy in copies:
        copy.wait()


def publish(*arrays):
    anywhere = pl.BlockSpec(memory_space=pl.ANY)
    return pl.pallas_call(
        publish_kernel,
        out_shape=[jax.ShapeDtypeStruct(a.shape, a.dtype) for a in arrays],
        in_specs=[anywhere] * 4,
        out_specs=[anywhere] * 4,
        scratch_shapes=[pltpu.SemaphoreType.DMA((4,))],
    )(*arrays)


def shards(frames, codebook, linear_map, code_tile, code_offset, reinit_source):
    commitment, nearest, gradient, fresh, used, over = exchange(
        frames,
        codebook,
        linear_map,
        code_tile.reshape(1, ROWS),
        code_offset.reshape(1, ROWS),
        reinit_source.reshape(1, ROWS),
    )

    def whole_gather():
        here = lax.axis_index("narrow")
        owner = reinit_source >> 10
        row = reinit_source & (ROWS - 1)
        result = jnp.where((owner == here)[:, None], frames[row], codebook)
        for shift in range(1, 4):
            theirs = lax.ppermute(frames, "narrow", [(j, (j - shift) % 4) for j in range(4)])
            result = jnp.where((owner == lax.rem(here + shift, 4))[:, None], theirs[row], result)
        return jnp.where(used.reshape(ROWS, 1) > 0.0, codebook, result)

    new_codebook = lax.cond(over[0, 0] > 0, whole_gather, lambda: fresh)
    commitment, nearest, gradient, new_codebook = publish(commitment, nearest, gradient, new_codebook)
    return commitment.reshape(ROWS), nearest.reshape(ROWS), gradient, new_codebook


def solution(mesh):
    placed = (
        P(("wide", "narrow"), None),
        P(("wide", "narrow"), None),
        P(),
        P(("wide", "narrow"), None),
        P(("wide", "narrow")),
        P(("wide", "narrow")),
    )
    return jax.shard_map(
        shards,
        mesh=mesh,
        in_specs=placed,
        out_specs=(
            P(("wide", "narrow")),
            P(("wide", "narrow")),
            P("wide", None),
            P(("wide", "narrow"), None),
        ),
        check_vma=False,
    )
```
